32 devices in a mesh: groups: 2 (over x), expert: 16 (over z, y, core).
Axes of the slice: x: 2, y: 2, z: 4, core: 2. Of those that a mesh axis runs over, the one named last changes fastest.
Arguments:
- tokens: bfloat16 [4096, 3584], P(('groups', 'expert')), parts along dimension 0, may hold values from -6 to 6
- expert_ids: int32 [4096, 2], P(('groups', 'expert')), parts along dimension 0, may hold values from 0 to 3, all different within a row; in each aligned block of 128 rows (0 to 127, 128 to 255, ...) at most 80 rows name the same one
- gate_weights: float32 [4096, 2], P(('groups', 'expert')), parts along dimension 0, may hold values from 0.5 to 2.5
- w_gate: bfloat16 [16, 3584, 512], P('expert'), may hold values from -0.09375 to 0.09375
- w_up: bfloat16 [16, 3584, 512], P('expert'), may hold values from -0.09375 to 0.09375
- w_down: bfloat16 [16, 512, 3584], P('expert'), may hold values from -0.125 to 0.125
Outputs:
- moe_output: bfloat16 [4096, 3584], P(('groups', 'expert')), parts along dimension 0
The draws below stay inside these ranges and needn't reach their ends.
There are 2 independent parts, one for each index of `groups`. The reference program is written for one: setup_inputs(seed, part) draws one part's arguments, and reference() takes and returns one part's arrays. A program takes and returns all parts, laid end to end along the dimension named above; an argument that names none is the same for every part. Nothing has to cross between parts.
Inputs may be any that keep to these rules, and one draw needn't show every extreme that they name: `expert_ids`: each row names 2 different experts. Among the rows of one device no expert is named by more than 80 rows, and in every draw some device has an expert named by exactly 80 of its rows.
All inputs are finite; a program needn't handle non-finite values.
Results may differ from the reference program's by a relative error of at most 0.0057.
Values may be sent and summed in bfloat16 or wider, within the bound.
No kernel may reach another device: no remote copies, remote signals or barrier semaphores. Data moves between devices by JAX's collectives and lax.ppermute only.
A program may use at most 128 MiB of HBM per device.

```python
import math
import jax
import jax.numpy as jnp
import numpy as np
from jax import lax

D = 3584
FF = 2048
FF_DEV = 512
TOP = 2
TOK_DEV = 128
SHARDS = 4
EXPERTS = 4
CAP = 80
TOKENS = 2048
N_EXPERT = 16


def block_scale(stream_key, dims, shards, smallest, largest):
    loudness = 1.0
    for position, blocks in shards:
        steps = jax.random.uniform(jax.random.fold_in(jax.random.fold_in(stream_key, 6), position), (blocks,), jnp.float32, smallest / len(shards), largest / len(shards))
        loudness = loudness * jnp.repeat(jnp.exp(steps), dims[position] // blocks).reshape((-1,) + (1,) * (len(dims) - 1 - position))
    return loudness


def deal_out(key, own, number, rows, number_of, top, most, skew):
    sequence = jax.random.permutation(key, number_of)
    packed, ordinary = shares(number_of, rows * top, most, skew, True), shares(number_of, rows * top, most, skew, False)
    places = jnp.arange(number_of)

    def named(sizes, turn):
        used = int((sizes > 0).sum())
        fixed = max(1, used // 4)
        passed = fixed + (places - fixed + turn * (used - fixed)) % max(1, number_of - fixed)
        return jnp.zeros((number_of,), jnp.int32).at[sequence[jnp.where(places < fixed, places, passed)]].set(jnp.asarray(sizes, jnp.int32))

    sizes = jnp.where(number % 4 == 0, named(packed, number // 4), named(ordinary, number - number // 4 - 1))
    mixed = jax.random.permutation(jax.random.fold_in(own, 3), number_of)
    donor, sink = mixed[0:number_of // 2 * 2:2], mixed[1:number_of // 2 * 2:2]
    room = jnp.minimum(sizes[donor] - 1, most - sizes[sink]) // 2
    room = jnp.where((donor == sequence[0]) | (sink == sequence[0]) | (sizes[sink] == 0), 0, jnp.maximum(room, 0))
    passed = jax.random.randint(jax.random.fold_in(own, 4), (number_of // 2,), 0, 1 << 20) % (room + 1)
    sizes = sizes.at[donor].add(-passed).at[sink].add(passed)
    items = jnp.searchsorted(jnp.cumsum(sizes), jnp.arange(rows * top), side="right").astype(jnp.int32)
    table = items.reshape(top, rows).T
    table = table[jax.random.permutation(jax.random.fold_in(own, 1), rows)]
    turn = jax.random.randint(jax.random.fold_in(own, 2), (rows, 1), 0, top)
    return jnp.take_along_axis(table, (jnp.arange(top)[None, :] + turn) % top, axis=1)


def shares(count, total, reach, lean, full):
    portions = [(1 << 20) // math.isqrt(grade ** lean) + 1 for grade in range(1, count + 1)]
    largest = reach if full else min(reach, max(-(-total // count), total * portions[0] // sum(portions)))
    least = 1 if total - largest >= count - 1 else 0
    given, rest = [largest] + [least] * (count - 1), total - largest - least * (count - 1)
    while rest > 0:
        candidates = [i for i in range(1, count) if given[i] < largest] or [i for i in range(1, count) if given[i] < reach]
        mass, left = sum([portions[i] for i in candidates]), rest
        for i in candidates:
            addition = min(reach - given[i], max(1, left * portions[i] // mass), rest)
            given[i] = given[i] + addition
            rest = rest - addition
    return np.array(given)


def bell_draw(key, dims, deviation, most, split=(), held_as=jnp.bfloat16):
    array = deviation * jax.random.normal(key, dims, jnp.float32)
    if split:
        array = array * block_scale(key, dims, split, -0.22, 0.18)
    return jnp.clip(array, -most, most).astype(held_as)


def setup_inputs(seed: int = 0, part: int = 0) -> dict:
    arg_keys = jax.random.split(jax.random.key(seed), 7)
    part_keys = jax.random.split(jax.random.fold_in(arg_keys[6], part), 7)
    tokens = bell_draw(part_keys[0], (TOKENS, D), 1.0, 6.0, ((0, 16),))
    expert_ids_keys = jax.random.split(jax.random.fold_in(part_keys[1], 1), TOKENS // TOK_DEV)
    expert_ids_turns = jax.random.permutation(jax.random.fold_in(part_keys[1], 3), TOKENS // TOK_DEV)
    expert_ids = jax.vmap(lambda own, number: deal_out(jax.random.fold_in(part_keys[1], 2), own, number, TOK_DEV, EXPERTS, TOP, CAP, 1))(expert_ids_keys, expert_ids_turns).reshape((TOKENS, TOP))
    gate_weights = jnp.clip(0.5 + 2.0 * jax.random.uniform(part_keys[2], (TOKENS, TOP), jnp.float32) ** block_scale(part_keys[2], (TOKENS, TOP), ((0, 16),), -0.2, 0.2), 0.5, 2.5)
    w_gate = bell_draw(arg_keys[3], (N_EXPERT, D, FF_DEV), D ** -0.5, 0.09375, ((0, 16),))
    w_up = bell_draw(arg_keys[4], (N_EXPERT, D, FF_DEV), D ** -0.5, 0.09375, ((0, 16),))
    w_down = bell_draw(arg_keys[5], (N_EXPERT, FF_DEV, D), FF ** -0.5, 0.125, ((0, 16),))
    return dict(tokens=tokens, expert_ids=expert_ids, gate_weights=gate_weights, w_gate=w_gate, w_up=w_up, w_down=w_down)


def reference(tokens, expert_ids, gate_weights, w_gate, w_up, w_down):
    gate_full = w_gate.reshape(EXPERTS, SHARDS, D, FF_DEV).transpose(0, 2, 1, 3).reshape(EXPERTS, D, FF)
    up_full = w_up.reshape(EXPERTS, SHARDS, D, FF_DEV).transpose(0, 2, 1, 3).reshape(EXPERTS, D, FF)
    down_full = w_down.reshape(EXPERTS, FF, D)
    flat_ids = expert_ids.reshape(-1).astype(jnp.int32)
    most_rows = N_EXPERT * CAP

    def per_expert(totals, expert):
        sort_key = jnp.where(flat_ids == expert, 0, 1).astype(jnp.int32)
        route_order = jnp.argsort(sort_key, stable=True)[:most_rows].astype(jnp.int32)
        is_routed = flat_ids[route_order] == expert
        picked = tokens[route_order // TOP]
        gate_proj = jnp.dot(picked, gate_full[expert], preferred_element_type=jnp.float32)
        up_proj = jnp.dot(picked, up_full[expert], preferred_element_type=jnp.float32)
        hidden = (jax.nn.silu(gate_proj) * up_proj).astype(jnp.bfloat16)
        result = jnp.dot(hidden, down_full[expert], preferred_element_type=jnp.float32)
        rounded = lax.optimization_barrier(result.astype(jnp.bfloat16)).astype(jnp.float32)
        totals = totals.at[route_order].add(jnp.where(is_routed[:, None], rounded, jnp.float32(0.0)))
        return totals, None

    start_rows = jnp.zeros((TOKENS * TOP, D), jnp.float32)
    totals, unused = lax.scan(per_expert, start_rows, jnp.arange(EXPERTS, dtype=jnp.int32))
    weighted = totals.reshape(TOKENS, TOP, D) * gate_weights.astype(jnp.float32)[:, :, None]
    return jnp.sum(weighted, axis=1).astype(jnp.bfloat16)
```

```python
import jax
import jax.numpy as jnp
from jax import lax
from jax.sharding import PartitionSpec as P

FF = 2048
BF = jnp.bfloat16
F32 = jnp.float32


def local(tokens, expert_ids, gate_weights, w_gate, w_up, w_down):
    tok_rows, features = tokens.shape
    routes = expert_ids.shape[1]
    devices = lax.axis_size("expert")
    shards = FF // w_gate.shape[2]
    experts = devices // shards
    capacity = shards * (
        (5 * tok_rows * routes * shards + 4 * devices * shards - 1) // (4 * devices * shards)
    )
    me = lax.axis_index("expert") // shards

    def move(x, to):
        return lax.ppermute(x, "expert", [(d, to(d)) for d in range(devices)])

    def turn(x, k):
        return move(x, lambda d: (d + k * shards) % devices) if k % experts else x

    def chip(x):
        return move(x, lambda d: d ^ 2)

    def core(x):
        return move(x, lambda d: d ^ 1)

    named = (expert_ids[:, :, None] == jnp.arange(experts, dtype=jnp.int32)).astype(F32)
    both = jnp.sum(named, axis=1)
    earlier = jnp.tril(jnp.ones((tok_rows, tok_rows), F32), -1)
    slot = jnp.dot(earlier, both, preferred_element_type=F32)
    slots = jnp.arange(capacity, dtype=F32)

    def dispatch(k):
        e = (me + k) % experts
        hot = lax.dynamic_index_in_dim(both, e, 1, keepdims=False)
        at = lax.dynamic_index_in_dim(slot, e, 1, keepdims=False)
        pick = jnp.where((at[None, :] == slots[:, None]) & (hot[None, :] > 0), 1.0, 0.0).astype(BF)
        return jnp.dot(pick, tokens, preferred_element_type=F32).astype(BF)

    def ffn(rows):
        gate = jnp.dot(rows, w_gate[0], preferred_element_type=F32)
        up = jnp.dot(rows, w_up[0], preferred_element_type=F32)
        hidden = (jax.nn.silu(gate) * up).astype(BF)
        return jnp.dot(hidden, w_down[0], preferred_element_type=F32)

    def expert(own):
        other = chip(own)
        mate_own, mate_other = core(own), core(other)
        part = ffn(jnp.concatenate([own, other, mate_own, mate_other]))
        two = part[: 2 * capacity] + core(part[2 * capacity :].astype(BF)).astype(F32)
        return (two[:capacity] + chip(two[capacity:].astype(BF)).astype(F32)).astype(BF)

    def combine(k, back):
        e = (me + k) % experts
        hot = lax.dynamic_index_in_dim(named, e, 2, keepdims=False)
        at = lax.dynamic_index_in_dim(slot, e, 1, keepdims=False)
        pick = jnp.where((at[:, None] == slots[None, :]), 1.0, 0.0).astype(BF)
        weight = jnp.sum(hot * gate_weights, axis=1)
        return weight[:, None] * jnp.dot(pick, back, preferred_element_type=F32)

    total = 0.0
    for k in range(experts):
        back = turn(expert(turn(dispatch(k), k)), -k)
        total = total + combine(k, back)
    return total.astype(BF)


def solution(mesh):
    placed = (
        P(("groups", "expert"), None),
        P(("groups", "expert"), None),
        P(("groups", "expert"), None),
        P("expert", None, None),
        P("expert", None, None),
        P("expert", None, None),
    )
    return jax.shard_map(
        local, mesh=mesh, in_specs=placed, out_specs=P(("groups", "expert"), None), check_vma=False
    )
```

```python
import jax
import jax.numpy as jnp
from jax import lax
from jax.experimental import pallas as pl
from jax.experimental.pallas import tpu as pltpu
from jax.sharding import PartitionSpec as P

FF = 2048
BF = jnp.bfloat16
F32 = jnp.float32
HALF = 256
WIDE = 512


def ffn_kernel(a, b, c, d, wg, wu, wd, keep, send, rows, hidden, vg, vu, vd, sems):
    n = a.shape[0]
    units = wg.shape[1]
    copies = []
    for j in range(0, units, HALF):
        for src, dst in ((wg, vg), (wu, vu)):
            cols = pl.ds(j, HALF)
            copies.append(
                pltpu.make_async_copy(src.at[:, cols], dst.at[:, cols], sems.at[len(copies)])
            )
    copies.append(pltpu.make_async_copy(wd, vd, sems.at[len(copies)]))
    for copy in copies:
        copy.start()
    for i, piece in enumerate((a, b, c, d)):
        rows[i * n : (i + 1) * n, :] = piece[...]
    for i, j in enumerate(range(0, units, HALF)):
        copies[2 * i].wait()
        gate = jnp.dot(rows[...], vg[:, j : j + HALF], preferred_element_type=F32)
        copies[2 * i + 1].wait()
        up = jnp.dot(rows[...], vu[:, j : j + HALF], preferred_element_type=F32)
        hidden[:, j : j + HALF] = (gate / (1.0 + jnp.exp(-gate)) * up).astype(BF)
    copies[-1].wait()

    @pl.loop(0, vd.shape[1] // WIDE)
    def _(j):
        cols = pl.ds(pl.multiple_of(j * WIDE, WIDE), WIDE)
        part = jnp.dot(hidden[...], vd[:, cols], preferred_element_type=F32)
        keep[:, cols] = part[: 2 * n]
        send[:, cols] = part[2 * n :].astype(BF)


def ffn(pieces, wg, wu, wd):
    n, features = pieces[0].shape
    units = wg.shape[1]
    near = pl.BlockSpec(memory_space=pltpu.VMEM)
    far = pl.BlockSpec(memory_space=pl.ANY)
    return pl.pallas_call(
        ffn_kernel,
        out_shape=(
            jax.ShapeDtypeStruct((2 * n, features), F32),
            jax.ShapeDtypeStruct((2 * n, features), BF),
        ),
        in_specs=[near] * 4 + [far] * 3,
        out_specs=(near, near),
        scratch_shapes=[
            pltpu.VMEM((4 * n, features), BF),
            pltpu.VMEM((4 * n, units), BF),
            pltpu.VMEM((features, units), BF),
            pltpu.VMEM((features, units), BF),
            pltpu.VMEM((units, features), BF),
            pltpu.SemaphoreType.DMA((2 * units // HALF + 1,)),
        ],
        compiler_params=pltpu.CompilerParams(vmem_limit_bytes=30 * 2**20),
        cost_estimate=pl.CostEstimate(
            flops=24 * n * features * units, bytes_accessed=6 * features * units, transcendentals=0
        ),
    )(*pieces, wg, wu, wd)


def after(x, *done):
    done = [d for d in done if d is not None]
    return lax.optimization_barrier((x, *done))[0] if done else x


def local(tokens, expert_ids, gate_weights, w_gate, w_up, w_down):
    tok_rows, features = tokens.shape
    routes = expert_ids.shape[1]
    devices = lax.axis_size("expert")
    shards = FF // w_gate.shape[2]
    experts = devices // shards
    capacity = -(-5 * tok_rows * routes // (4 * experts))
    capacity = -(-capacity // 16) * 16
    me = lax.axis_index("expert") // shards
    wg, wu, wd = w_gate[0], w_up[0], w_down[0]

    def move(x, to):
        return lax.ppermute(x, "expert", [(d, to(d)) for d in range(devices)])

    def turn(x, k):
        return move(x, lambda d: (d + k * shards) % devices)

    def chip(x):
        return move(x, lambda d: d ^ 2)

    def core(x):
        return move(x, lambda d: d ^ 1)

    named = (expert_ids[:, :, None] == jnp.arange(experts, dtype=jnp.int32)).astype(F32)
    both = jnp.sum(named, axis=1)
    earlier = jnp.tril(jnp.ones((tok_rows, tok_rows), F32), -1)
    slot = jnp.dot(earlier, both, preferred_element_type=F32)

    def pack(chunk):
        k, first, size = chunk
        e = (me + k) % experts
        hot = lax.dynamic_index_in_dim(both, e, 1, keepdims=False)
        at = lax.dynamic_index_in_dim(slot, e, 1, keepdims=False)
        slots = jnp.arange(first, first + size, dtype=F32)
        pick = jnp.where((at[None, :] == slots[:, None]) & (hot[None, :] > 0), 1.0, 0.0).astype(BF)
        return jnp.dot(pick, tokens, preferred_element_type=F32).astype(BF)

    def combine(chunk, back):
        k, first, size = chunk
        e = (me + k) % experts
        hot = lax.dynamic_index_in_dim(named, e, 2, keepdims=False)
        at = lax.dynamic_index_in_dim(slot, e, 1, keepdims=False)
        slots = jnp.arange(first, first + size, dtype=F32)
        pick = jnp.where((at[:, None] == slots[None, :]), 1.0, 0.0).astype(BF)
        weight = jnp.sum(hot * gate_weights, axis=1)
        return weight[:, None] * jnp.dot(pick, back, preferred_element_type=F32)

    chunks = [(0, 0, capacity)]
    for k in range(1, (experts + 1) // 2):
        chunks += [(k, 0, capacity), (experts - k, 0, capacity)]
    if experts % 2 == 0:
        head = -(-capacity // 32) * 16
        chunks += [(experts // 2, 0, head)]
        if capacity > head:
            chunks += [(experts // 2, head, capacity - head)]
    count = len(chunks)
    lead = min(4, count)
    order = [("d", i) for i in range(lead)]
    back_next = 1
    for i in range(lead, count):
        order += [("r", back_next), ("d", i)]
        back_next += 1
    order += [("r", i) for i in range(back_next, count)] + [("r", 0)]

    z_last = y_last = None
    here, other, keeps, backs = {}, {}, {}, {}

    for i, chunk in enumerate(chunks):
        x = pack(chunk)
        if chunk[0]:
            x = z_last = turn(after(x, z_last), chunk[0])
        here[i] = x
    for what, i in order:
        if what == "d":
            other[i] = y_last = chip(after(here[i], y_last))
            pieces = (here[i], other[i], core(here[i]), core(other[i]))
            keep, send = ffn(pieces, wg, wu, wd)
            keeps[i] = keep + core(send).astype(F32)
        else:
            n = chunks[i][2]
            y_last = chip(after(keeps[i][n:].astype(BF), y_last))
            back = (keeps[i][:n] + y_last.astype(F32)).astype(BF)
            if chunks[i][0]:
                back = z_last = turn(after(back, z_last), -chunks[i][0])
            backs[i] = back
    total = 0.0
    for i, chunk in enumerate(chunks):
        total = total + combine(chunk, backs[i])
    return total.astype(BF)


def solution(mesh):
    placed = (
        P(("groups", "expert"), None),
        P(("groups", "expert"), None),
        P(("groups", "expert"), None),
        P("expert", None, None),
        P("expert", None, None),
        P("expert", None, None),
    )
    return jax.shard_map(
        local, mesh=mesh, in_specs=placed, out_specs=P(("groups", "expert"), None), check_vma=False
    )
```

```python
import jax
import jax.numpy as jnp
from jax import lax
from jax.experimental import pallas as pl
from jax.experimental.pallas import tpu as pltpu
from jax.sharding import PartitionSpec as P

FF = 2048
BF = jnp.bfloat16
F32 = jnp.float32


def load_kernel(wg, wu, wd, vg, vu, vd, sems):
    copies = [
        pltpu.make_async_copy(src, dst, sems.at[i])
        for i, (src, dst) in enumerate(((wg, vg), (wu, vu), (wd, vd)))
    ]
    for copy in copies:
        copy.start()
    for copy in copies:
        copy.wait()


def load(*weights):
    far = pl.BlockSpec(memory_space=pltpu.HBM)
    near = pl.BlockSpec(memory_space=pltpu.VMEM)
    return pl.pallas_call(
        load_kernel,
        out_shape=[jax.ShapeDtypeStruct(w.shape, w.dtype) for w in weights],
        in_specs=[far] * 3,
        out_specs=[near] * 3,
        scratch_shapes=[pltpu.SemaphoreType.DMA((3,))],
        compiler_params=pltpu.CompilerParams(vmem_limit_bytes=16 * 2**20),
        cost_estimate=pl.CostEstimate(flops=0, bytes_accessed=1024, transcendentals=0),
    )(*weights)


def ffn_kernel(a, b, vg, vu, vd, keep, send, rows, hidden):
    n = a.shape[0]
    rows[:n, :] = a[...]
    rows[n:, :] = b[...]
    gate = jnp.dot(rows[...], vg[...], preferred_element_type=F32)
    up = jnp.dot(rows[...], vu[...], preferred_element_type=F32)
    hidden[...] = (gate / (1.0 + jnp.exp(-gate)) * up).astype(BF)
    wide = vd.shape[1] // 2

    @pl.loop(0, 2)
    def _(j):
        cols = pl.ds(pl.multiple_of(j * wide, 128), wide)
        part = jnp.dot(hidden[...], vd[:, cols], preferred_element_type=F32)
        keep[:, cols] = part[:n]
        send[:, cols] = part[n:].astype(BF)


def ffn(mine, mate, wg, wu, wd):
    n, features = mine.shape
    units = wg.shape[1]
    near = pl.BlockSpec(memory_space=pltpu.VMEM)
    return pl.pallas_call(
        ffn_kernel,
        out_shape=(
            jax.ShapeDtypeStruct((n, features), F32),
            jax.ShapeDtypeStruct((n, features), BF),
        ),
        in_specs=[near] * 5,
        out_specs=(near,) * 2,
        scratch_shapes=[pltpu.VMEM((2 * n, features), BF), pltpu.VMEM((2 * n, units), BF)],
        compiler_params=pltpu.CompilerParams(vmem_limit_bytes=24 * 2**20),
        cost_estimate=pl.CostEstimate(
            flops=48 * n * features * units, bytes_accessed=6 * features * units, transcendentals=0
        ),
    )(mine, mate, wg, wu, wd)


def after(x, *done):
    done = [d for d in done if d is not None]
    return lax.optimization_barrier((x, *done))[0] if done else x


def local(tokens, expert_ids, gate_weights, w_gate, w_up, w_down):
    tok_rows, features = tokens.shape
    routes = expert_ids.shape[1]
    devices = lax.axis_size("expert")
    shards = FF // w_gate.shape[2]
    experts = devices // shards
    capacity = -(-5 * tok_rows * routes // (4 * experts))
    capacity = -(-capacity // 16) * 16
    me = lax.axis_index("expert") // shards

    def move(x, to):
        return lax.ppermute(x, "expert", [(d, to(d)) for d in range(devices)])

    def turn(x, k):
        return move(x, lambda d: (d + k * shards) % devices)

    def chip(x):
        return move(x, lambda d: d ^ 2)

    def core(x):
        return move(x, lambda d: d ^ 1)

    named = (expert_ids[:, :, None] == jnp.arange(experts, dtype=jnp.int32)).astype(F32)
    both = jnp.sum(named, axis=1)
    earlier = jnp.tril(jnp.ones((tok_rows, tok_rows), F32), -1)
    slot = jnp.dot(earlier, both, preferred_element_type=F32)

    def pack(chunk):
        k, first, size = chunk
        e = (me + k) % experts
        hot = lax.dynamic_index_in_dim(both, e, 1, keepdims=False)
        at = lax.dynamic_index_in_dim(slot, e, 1, keepdims=False)
        slots = jnp.arange(first, first + size, dtype=F32)
        pick = jnp.where((at[None, :] == slots[:, None]) & (hot[None, :] > 0), 1.0, 0.0).astype(BF)
        return jnp.dot(pick, tokens, preferred_element_type=F32).astype(BF)

    def combine(chunk, back):
        k, first, size = chunk
        e = (me + k) % experts
        hot = lax.dynamic_index_in_dim(named, e, 2, keepdims=False)
        at = lax.dynamic_index_in_dim(slot, e, 1, keepdims=False)
        slots = jnp.arange(first, first + size, dtype=F32)
        pick = jnp.where((at[:, None] == slots[None, :]), 1.0, 0.0).astype(BF)
        weight = jnp.sum(hot * gate_weights, axis=1)
        return weight[:, None] * jnp.dot(pick, back, preferred_element_type=F32)

    chunks = [(0, 0, capacity)]
    for k in range(1, (experts + 1) // 2):
        chunks += [(k, 0, capacity), (experts - k, 0, capacity)]
    if experts % 2 == 0:
        head = -(-capacity // 32) * 16
        chunks += [(experts // 2, 0, head)]
        if capacity > head:
            chunks += [(experts // 2, head, capacity - head)]
    count = len(chunks)
    live = {}

    def send_out(i):
        with jax.named_scope(f"zout{i}"):
            live["here", i] = turn(live["here", i], chunks[i][0])

    def cross(i):
        with jax.named_scope(f"yout{i}"):
            live["other", i] = chip(live["here", i])

    def work(i):
        mine = jnp.concatenate([live.pop(("here", i)), live.pop(("other", i))])
        with jax.named_scope(f"cout{i}"):
            mate = core(mine)
        with jax.named_scope(f"ffn{i}"):
            live["keep", i], live["send", i] = ffn(mine, mate, live["w", 0], live["w", 1], live["w", 2])

    def swap(i):
        with jax.named_scope(f"cback{i}"):
            live["got", i] = core(live.pop(("send", i)))

    def add(i):
        live["sum", i] = live.pop(("keep", i)) + live.pop(("got", i)).astype(F32)

    def cross_back(i):
        n = chunks[i][2]
        with jax.named_scope(f"yback{i}"):
            total = live.pop(("sum", i))
            got = chip(total[n:].astype(BF))
        live["back", i] = (total[:n] + got.astype(F32)).astype(BF)

    def cross_back_part(i, first, last):
        with jax.named_scope(f"ypart{i}"):
            total = live["sum", i]
            n = chunks[i][2]
            got = chip(total[n + first : n + last].astype(BF))
        live["part", i, first] = (total[first:last] + got.astype(F32)).astype(BF)

    def send_back(i):
        with jax.named_scope(f"zback{i}"):
            live["back", i] = turn(live["back", i], -chunks[i][0])

    def settle():
        keys = list(live)
        for key, value in zip(keys, lax.optimization_barrier([live[key] for key in keys])):
            live[key] = value

    for i, weight in enumerate(load(w_gate[0], w_up[0], w_down[0])):
        live["w", i] = weight
    for i, chunk in enumerate(chunks):
        live["here", i] = pack(chunk)
    if count == 5:
        send_out(1)
        cross(0)
        settle()
        send_out(2)
        cross(1)
        work(0)
        settle()
        send_out(3)
        cross(2)
        swap(0)
        work(1)
        settle()
        send_out(4)
        cross(3)
        swap(1)
        add(0)
        add(1)
        cross_back(1)
        work(2)
        settle()
        swap(2)
        add(2)
        send_back(1)
        cross(4)
        cross_back(2)
        work(3)
        settle()
        swap(3)
        add(3)
        send_back(2)
        cross_back(3)
        cross_back_part(0, 0, 32)
        work(4)
        settle()
        swap(4)
        add(4)
        send_back(3)
        cross_back(4)
        cross_back_part(0, 32, capacity)
        live["back", 0] = jnp.concatenate([live["part", 0, 0], live["part", 0, 32]])
        send_back(4)
    else:
        for i in range(count):
            if i:
                send_out(i)
            cross(i)
            work(i)
            swap(i)
            add(i)
            cross_back(i)
            if i:
                send_back(i)
    backs = [live["back", i] for i in range(count)]
    total = 0.0
    for i, chunk in enumerate(chunks):
        total = total + combine(chunk, backs[i])
    return total.astype(BF)


def solution(mesh):
    placed = (
        P(("groups", "expert"), None),
        P(("groups", "expert"), None),
        P(("groups", "expert"), None),
        P("expert", None, None),
        P("expert", None, None),
        P("expert", None, None),
    )
    return jax.shard_map(
        local, mesh=mesh, in_specs=placed, out_specs=P(("groups", "expert"), None), check_vma=False
    )
```

```python
import jax
import jax.numpy as jnp
from jax import lax
from jax.experimental import pallas as pl
from jax.experimental.pallas import tpu as pltpu
from jax.sharding import PartitionSpec as P

FF = 2048
BF = jnp.bfloat16
F32 = jnp.float32


def load_kernel(wg, wu, wd, vg, vu, vd, sems):
    copies = [
        pltpu.make_async_copy(src, dst, sems.at[i])
        for i, (src, dst) in enumerate(((wg, vg), (wu, vu), (wd, vd)))
    ]
    for copy in copies:
        copy.start()
    for copy in copies:
        copy.wait()


def load(*weights):
    far = pl.BlockSpec(memory_space=pltpu.HBM)
    near = pl.BlockSpec(memory_space=pltpu.VMEM)
    return pl.pallas_call(
        load_kernel,
        out_shape=[jax.ShapeDtypeStruct(w.shape, w.dtype) for w in weights],
        in_specs=[far] * 3,
        out_specs=[near] * 3,
        scratch_shapes=[pltpu.SemaphoreType.DMA((3,))],
        compiler_params=pltpu.CompilerParams(vmem_limit_bytes=16 * 2**20),
        cost_estimate=pl.CostEstimate(flops=0, bytes_accessed=1024, transcendentals=0),
    )(*weights)


def ffn_kernel(a, b, vg, vu, vd, keep, send, rows, hidden):
    n = a.shape[0]
    rows[:n, :] = a[...]
    rows[n:, :] = b[...]
    gate = jnp.dot(rows[...], vg[...], preferred_element_type=F32)
    up = jnp.dot(rows[...], vu[...], preferred_element_type=F32)
    hidden[...] = (gate / (1.0 + jnp.exp(-gate)) * up).astype(BF)
    wide = vd.shape[1] // 2

    @pl.loop(0, 2)
    def _(j):
        cols = pl.ds(pl.multiple_of(j * wide, 128), wide)
        part = jnp.dot(hidden[...], vd[:, cols], preferred_element_type=F32)
        keep[:, cols] = part[:n]
        send[:, cols] = part[n:].astype(BF)


def ffn(mine, mate, wg, wu, wd):
    n, features = mine.shape
    units = wg.shape[1]
    near = pl.BlockSpec(memory_space=pltpu.VMEM)
    return pl.pallas_call(
        ffn_kernel,
        out_shape=(
            jax.ShapeDtypeStruct((n, features), F32),
            jax.ShapeDtypeStruct((n, features), BF),
        ),
        in_specs=[near] * 5,
        out_specs=(near,) * 2,
        scratch_shapes=[pltpu.VMEM((2 * n, features), BF), pltpu.VMEM((2 * n, units), BF)],
        compiler_params=pltpu.CompilerParams(vmem_limit_bytes=24 * 2**20),
        cost_estimate=pl.CostEstimate(
            flops=48 * n * features * units, bytes_accessed=6 * features * units, transcendentals=0
        ),
    )(mine, mate, wg, wu, wd)


def after(x, *done):
    done = [d for d in done if d is not None]
    return lax.optimization_barrier((x, *done))[0] if done else x


def local(tokens, expert_ids, gate_weights, w_gate, w_up, w_down):
    tok_rows, features = tokens.shape
    routes = expert_ids.shape[1]
    devices = lax.axis_size("expert")
    shards = FF // w_gate.shape[2]
    experts = devices // shards
    capacity = -(-5 * tok_rows * routes // (4 * experts))
    capacity = -(-capacity // 16) * 16
    me = lax.axis_index("expert") // shards

    def move(x, to):
        return lax.ppermute(x, "expert", [(d, to(d)) for d in range(devices)])

    def turn(x, k):
        return move(x, lambda d: (d + k * shards) % devices)

    def chip(x):
        return move(x, lambda d: d ^ 2)

    def core(x):
        return move(x, lambda d: d ^ 1)

    named = (expert_ids[:, :, None] == jnp.arange(experts, dtype=jnp.int32)).astype(F32)
    both = jnp.sum(named, axis=1)
    earlier = jnp.tril(jnp.ones((tok_rows, tok_rows), F32), -1)
    slot = jnp.dot(earlier, both, preferred_element_type=F32)

    def pack(chunk):
        k, first, size = chunk
        e = (me + k) % experts
        hot = lax.dynamic_index_in_dim(both, e, 1, keepdims=False)
        at = lax.dynamic_index_in_dim(slot, e, 1, keepdims=False)
        slots = jnp.arange(first, first + size, dtype=F32)
        pick = jnp.where((at[None, :] == slots[:, None]) & (hot[None, :] > 0), 1.0, 0.0).astype(BF)
        return jnp.dot(pick, tokens, preferred_element_type=F32).astype(BF)

    def combine(chunk, back):
        k, first, size = chunk
        e = (me + k) % experts
        hot = lax.dynamic_index_in_dim(named, e, 2, keepdims=False)
        at = lax.dynamic_index_in_dim(slot, e, 1, keepdims=False)
        slots = jnp.arange(first, first + size, dtype=F32)
        pick = jnp.where((at[:, None] == slots[None, :]), 1.0, 0.0).astype(BF)
        weight = jnp.sum(hot * gate_weights, axis=1)
        return weight[:, None] * jnp.dot(pick, back, preferred_element_type=F32)

    chunks = [(0, 0, capacity)]
    for k in range(1, (experts + 1) // 2):
        chunks += [(k, 0, capacity), (experts - k, 0, capacity)]
    if experts % 2 == 0:
        head = -(-capacity // 32) * 16
        chunks += [(experts // 2, 0, head)]
        if capacity > head:
            chunks += [(experts // 2, head, capacity - head)]
    count = len(chunks)
    live = {}

    def send_out(i):
        with jax.named_scope(f"zout{i}"):
            live["here", i] = turn(live["here", i], chunks[i][0])

    def cross(i):
        with jax.named_scope(f"yout{i}"):
            live["other", i] = chip(live["here", i])

    def work(i):
        mine = jnp.concatenate([live.pop(("here", i)), live.pop(("other", i))])
        with jax.named_scope(f"cout{i}"):
            mate = core(mine)
        with jax.named_scope(f"ffn{i}"):
            live["keep", i], live["send", i] = ffn(mine, mate, live["w", 0], live["w", 1], live["w", 2])

    def swap(i):
        with jax.named_scope(f"cback{i}"):
            live["got", i] = core(live.pop(("send", i)))

    def add(i):
        live["sum", i] = live.pop(("keep", i)) + live.pop(("got", i)).astype(F32)

    def cross_back(i):
        n = chunks[i][2]
        with jax.named_scope(f"yback{i}"):
            total = live.pop(("sum", i))
            got = chip(total[n:].astype(BF))
        live["back", i] = (total[:n] + got.astype(F32)).astype(BF)

    def cross_back_part(i, first, last):
        with jax.named_scope(f"ypart{i}"):
            total = live["sum", i]
            n = chunks[i][2]
            got = chip(total[n + first : n + last].astype(BF))
        live["part", i, first] = (total[first:last] + got.astype(F32)).astype(BF)

    def send_back(i):
        with jax.named_scope(f"zback{i}"):
            live["back", i] = turn(live["back", i], -chunks[i][0])

    def settle():
        keys = list(live)
        for key, value in zip(keys, lax.optimization_barrier([live[key] for key in keys])):
            live[key] = value

    for i, weight in enumerate(load(w_gate[0], w_up[0], w_down[0])):
        live["w", i] = weight
    for i, chunk in enumerate(chunks):
        live["here", i] = pack(chunk)
    if count == 5:
        send_out(1)
        cross(0)
        settle()
        send_out(2)
        cross(1)
        work(0)
        send_out(3)
        cross(2)
        swap(0)
        work(1)
        settle()
        send_out(4)
        cross(3)
        swap(1)
        add(0)
        add(1)
        cross_back(1)
        work(2)
        settle()
        swap(2)
        add(2)
        send_back(1)
        cross(4)
        cross_back(2)
        work(3)
        settle()
        swap(3)
        add(3)
        send_back(2)
        cross_back(3)
        work(4)
        swap(4)
        add(4)
        send_back(3)
        cross_back(4)
        live["sum", 0], live["back", 4] = lax.optimization_barrier((live["sum", 0], live["back", 4]))
        cross_back(0)
        send_back(4)
    else:
        for i in range(count):
            if i:
                send_out(i)
            cross(i)
            work(i)
            swap(i)
            add(i)
            cross_back(i)
            if i:
                send_back(i)
    backs = [live["back", i] for i in range(count)]
    total = 0.0
    for i, chunk in enumerate(chunks):
        total = total + combine(chunk, backs[i])
    return total.astype(BF)


def solution(mesh):
    placed = (
        P(("groups", "expert"), None),
        P(("groups", "expert"), None),
        P(("groups", "expert"), None),
        P("expert", None, None),
        P("expert", None, None),
        P("expert", None, None),
    )
    return jax.shard_map(
        local, mesh=mesh, in_specs=placed, out_specs=P(("groups", "expert"), None), check_vma=False
    )
```

```python
import jax
import jax.numpy as jnp
from jax import lax
from jax.experimental import pallas as pl
from jax.experimental.pallas import tpu as pltpu
from jax.sharding import PartitionSpec as P

FF = 2048
BF = jnp.bfloat16
F32 = jnp.float32


def load_kernel(wg, wu, wd, vg, vu, vd, sems):
    copies = [
        pltpu.make_async_copy(src, dst, sems.at[i])
        for i, (src, dst) in enumerate(((wg, vg), (wu, vu), (wd, vd)))
    ]
    for copy in copies:
        copy.start()
    for copy in copies:
        copy.wait()


def load(*weights):
    far = pl.BlockSpec(memory_space=pltpu.HBM)
    near = pl.BlockSpec(memory_space=pltpu.VMEM)
    return pl.pallas_call(
        load_kernel,
        out_shape=[jax.ShapeDtypeStruct(w.shape, w.dtype) for w in weights],
        in_specs=[far] * 3,
        out_specs=[near] * 3,
        scratch_shapes=[pltpu.SemaphoreType.DMA((3,))],
        compiler_params=pltpu.CompilerParams(vmem_limit_bytes=16 * 2**20),
        cost_estimate=pl.CostEstimate(flops=0, bytes_accessed=1024, transcendentals=0),
    )(*weights)


def ffn_kernel(a, b, vg, vu, vd, keep, send, rows, hidden):
    n = a.shape[0]
    rows[:n, :] = a[...]
    rows[n:, :] = b[...]
    gate = jnp.dot(rows[...], vg[...], preferred_element_type=F32)
    up = jnp.dot(rows[...], vu[...], preferred_element_type=F32)
    hidden[...] = (gate / (1.0 + jnp.exp(-gate)) * up).astype(BF)
    wide = vd.shape[1] // 2

    @pl.loop(0, 2)
    def _(j):
        cols = pl.ds(pl.multiple_of(j * wide, 128), wide)
        part = jnp.dot(hidden[...], vd[:, cols], preferred_element_type=F32)
        keep[:, cols] = part[:n]
        send[:, cols] = part[n:].astype(BF)


def ffn(mine, mate, wg, wu, wd):
    n, features = mine.shape
    units = wg.shape[1]
    near = pl.BlockSpec(memory_space=pltpu.VMEM)
    return pl.pallas_call(
        ffn_kernel,
        out_shape=(
            jax.ShapeDtypeStruct((n, features), F32),
            jax.ShapeDtypeStruct((n, features), BF),
        ),
        in_specs=[near] * 5,
        out_specs=(near,) * 2,
        scratch_shapes=[pltpu.VMEM((2 * n, features), BF), pltpu.VMEM((2 * n, units), BF)],
        compiler_params=pltpu.CompilerParams(vmem_limit_bytes=24 * 2**20),
        cost_estimate=pl.CostEstimate(
            flops=48 * n * features * units, bytes_accessed=6 * features * units, transcendentals=0
        ),
    )(mine, mate, wg, wu, wd)


def after(x, *done):
    done = [d for d in done if d is not None]
    return lax.optimization_barrier((x, *done))[0] if done else x


def local(tokens, expert_ids, gate_weights, w_gate, w_up, w_down):
    tok_rows, features = tokens.shape
    routes = expert_ids.shape[1]
    devices = lax.axis_size("expert")
    shards = FF // w_gate.shape[2]
    experts = devices // shards
    capacity = -(-5 * tok_rows * routes // (4 * experts))
    capacity = -(-capacity // 16) * 16
    me = lax.axis_index("expert") // shards

    def move(x, to):
        return lax.ppermute(x, "expert", [(d, to(d)) for d in range(devices)])

    def turn(x, k):
        return move(x, lambda d: (d + k * shards) % devices)

    def chip(x):
        return move(x, lambda d: d ^ 2)

    def core(x):
        return move(x, lambda d: d ^ 1)

    named = (expert_ids[:, :, None] == jnp.arange(experts, dtype=jnp.int32)).astype(F32)
    both = jnp.sum(named, axis=1)
    earlier = jnp.tril(jnp.ones((tok_rows, tok_rows), F32), -1)
    slot = jnp.dot(earlier, both, preferred_element_type=F32)

    def pack(chunk):
        k, first, size = chunk
        e = (me + k) % experts
        hot = lax.dynamic_index_in_dim(both, e, 1, keepdims=False)
        at = lax.dynamic_index_in_dim(slot, e, 1, keepdims=False)
        slots = jnp.arange(first, first + size, dtype=F32)
        pick = jnp.where((at[None, :] == slots[:, None]) & (hot[None, :] > 0), 1.0, 0.0).astype(BF)
        return jnp.dot(pick, tokens, preferred_element_type=F32).astype(BF)

    def combine(chunk, back):
        k, first, size = chunk
        e = (me + k) % experts
        hot = lax.dynamic_index_in_dim(named, e, 2, keepdims=False)
        at = lax.dynamic_index_in_dim(slot, e, 1, keepdims=False)
        slots = jnp.arange(first, first + size, dtype=F32)
        pick = jnp.where((at[:, None] == slots[None, :]), 1.0, 0.0).astype(BF)
        weight = jnp.sum(hot * gate_weights, axis=1)
        return weight[:, None] * jnp.dot(pick, back, preferred_element_type=F32)

    chunks = [(0, 0, capacity)]
    for k in range(1, (experts + 1) // 2):
        chunks += [(k, 0, capacity), (experts - k, 0, capacity)]
    if experts % 2 == 0:
        head = -(-capacity // 32) * 16
        chunks += [(experts // 2, 0, head)]
        if capacity > head:
            chunks += [(experts // 2, head, capacity - head)]
    count = len(chunks)
    live = {}

    def send_out(i):
        with jax.named_scope(f"zout{i}"):
            live["here", i] = turn(live["here", i], chunks[i][0])

    def cross(i):
        with jax.named_scope(f"yout{i}"):
            live["other", i] = chip(live["here", i])

    def work(i):
        mine = jnp.concatenate([live.pop(("here", i)), live.pop(("other", i))])
        with jax.named_scope(f"cout{i}"):
            mate = core(mine)
        with jax.named_scope(f"ffn{i}"):
            live["keep", i], live["send", i] = ffn(mine, mate, live["w", 0], live["w", 1], live["w", 2])

    def swap(i):
        with jax.named_scope(f"cback{i}"):
            live["got", i] = core(live.pop(("send", i)))

    def add(i):
        live["sum", i] = live.pop(("keep", i)) + live.pop(("got", i)).astype(F32)

    def cross_back(i):
        n = chunks[i][2]
        with jax.named_scope(f"yback{i}"):
            total = live.pop(("sum", i))
            got = chip(total[n:].astype(BF))
        live["back", i] = (total[:n] + got.astype(F32)).astype(BF)

    def cross_back_part(i, first, last):
        with jax.named_scope(f"ypart{i}"):
            total = live["sum", i]
            n = chunks[i][2]
            got = chip(total[n + first : n + last].astype(BF))
        live["part", i, first] = (total[first:last] + got.astype(F32)).astype(BF)

    def send_back(i):
        with jax.named_scope(f"zback{i}"):
            live["back", i] = turn(live["back", i], -chunks[i][0])

    def settle():
        keys = list(live)
        for key, value in zip(keys, lax.optimization_barrier([live[key] for key in keys])):
            live[key] = value

    for i, weight in enumerate(load(w_gate[0], w_up[0], w_down[0])):
        live["w", i] = weight
    for i, chunk in enumerate(chunks):
        live["here", i] = pack(chunk)
    if count == 5:
        send_out(1)
        cross(0)
        settle()
        send_out(2)
        cross(1)
        work(0)
        send_out(3)
        cross(2)
        swap(0)
        work(1)
        settle()
        send_out(4)
        cross(3)
        swap(1)
        add(0)
        add(1)
        cross_back(1)
        work(2)
        settle()
        swap(2)
        add(2)
        send_back(1)
        cross(4)
        cross_back(2)
        work(3)
        settle()
        swap(3)
        add(3)
        send_back(2)
        cross_back(3)
        work(4)
        swap(4)
        add(4)
        send_back(3)
        cross_back(4)
        live["sum", 0], live["back", 4] = lax.optimization_barrier((live["sum", 0], live["back", 4]))
        cross_back(0)
        send_back(4)
    else:
        for i in range(count):
            if i:
                send_out(i)
            cross(i)
            work(i)
            swap(i)
            add(i)
            cross_back(i)
            if i:
                send_back(i)
    backs = [live["back", i] for i in range(count)]
    total = 0.0
    late = max(1, count - 2)
    for i in [*range(1, late), 0, *range(late, count)]:
        total = total + combine(chunks[i], backs[i])
    return total.astype(BF)


def solution(mesh):
    placed = (
        P(("groups", "expert"), None),
        P(("groups", "expert"), None),
        P(("groups", "expert"), None),
        P("expert", None, None),
        P("expert", None, None),
        P("expert", None, None),
    )
    return jax.shard_map(
        local, mesh=mesh, in_specs=placed, out_specs=P(("groups", "expert"), None), check_vma=False
    )
```
